32 devices in a mesh: visit: 8 (over z, core), patch: 4 (over y, x).
Axes of the slice: x: 2, y: 2, z: 4, core: 2. Of those that a mesh axis runs over, the one named last changes fastest.
Arguments:
- images: bfloat16 [8, 1024, 4096], P('visit', 'patch'), may hold values from -6 to 6
- psf_taps: bfloat16 [8, 2, 13], P('visit'), may hold values from 0.019897461 to 0.19921875
- exposure_weights: float32 [8], P('visit'), may hold values from 0.5 to 8
- dest_patch: int32 [8, 8, 32], P('visit', 'patch'), may hold values from -1 to 3, as said below
- dest_cell: int32 [8, 8, 32], P('visit', 'patch'), may hold values from -1 to 63, as said below
- shift_class: int32 [8, 2, 8, 32], P('visit', None, 'patch'), may hold values from 0 to 7
Outputs:
- coadd: float32 [4, 64, 128, 128], P('patch', 'visit')
- weight_map: float32 [4, 64], P('patch', 'visit')
The draws below stay inside these ranges and needn't reach their ends.
Inputs may be any that keep to these rules, and one draw needn't show every extreme that they name: `dest_patch`: within one exposure all tiles move to sky cells by one whole-cell offset of at most 2 cells along each direction, so distinct tiles land in distinct cells; the patch of cell row u and column w is (u // 8) * 4 + w // 8. Of the 64 tiles in one exposure's band of 256 rows, at most 16 fall in any one patch. `dest_cell`: cell index (u % 8) * 8 + w % 8; -1 exactly where dest_patch is -1.
All inputs are finite; a program needn't handle non-finite values.
Results may differ from the reference program's by a relative error of at most 0.0004.
The reference program's roundings to bfloat16 on the way count: a program that leaves them out, or rounds other values in their place, can miss the bound.
Values may be sent and summed in bfloat16 or wider, within the bound.
A program may use at most 128 MiB of HBM per device.

```python
import math
import jax
import jax.numpy as jnp
from jax import lax

TILE = 128
KTAPS = 13
SHIFTS = 8
PCELLS = 8
COLS = 4096
ROWS = 1024
EXPOS = 8
PATCHES = 4
CELLS = 64


def sky_cells(key):
    reach = 2
    shift_y = jax.random.randint(jax.random.fold_in(key, 11), (EXPOS, 1, 1), -reach, reach + 1)
    shift_x = jax.random.randint(jax.random.fold_in(key, 12), (EXPOS, 1, 1), -reach, reach + 1)
    grid_rows = ROWS // TILE
    grid_cols = COLS // TILE
    cell_y = jnp.arange(grid_rows, dtype=jnp.int32)[None, :, None] + shift_y
    cell_x = jnp.arange(grid_cols, dtype=jnp.int32)[None, None, :] + shift_x
    inside = (cell_y >= 0) & (cell_y < grid_rows) & (cell_x >= 0) & (cell_x < grid_cols)
    patch = cell_y // PCELLS * (grid_cols // PCELLS) + cell_x // PCELLS
    cell = cell_y % PCELLS * PCELLS + cell_x % PCELLS
    return (jnp.where(inside, patch, -1).astype(jnp.int32), jnp.where(inside, cell, -1).astype(jnp.int32))


def draw_dest_patch(key, part):
    return sky_cells(key)[0]


def draw_dest_cell(key, part):
    return sky_cells(key)[1]


def touch_ends(values, key, least, high):
    place = [jax.random.randint(jax.random.fold_in(key, axis), (), 0, length) for axis, length in enumerate(values.shape)]
    longest = values.shape.index(max(values.shape))
    next_to = place[:longest] + [(place[longest] + 1) % values.shape[longest]] + place[longest + 1:]
    return values.at[tuple(place)].set(least).at[tuple(next_to)].set(high)


def shard_levels(rng, dims, cuts, smallest, top_value):
    loudness = 1.0
    for position, parts in cuts:
        draws = jax.random.uniform(jax.random.fold_in(jax.random.fold_in(rng, 6), position), (parts,), jnp.float32, smallest / len(cuts), top_value / len(cuts))
        loudness = loudness * jnp.repeat(jnp.exp(draws), dims[position] // parts).reshape((-1,) + (1,) * (len(dims) - 1 - position))
    return loudness


def gaussian(key, dims, deviation, bound, shards=(), kind=jnp.bfloat16):
    gain = shard_levels(key, dims, shards, -0.22, 0.18) if shards else 1.0
    array = jax.random.normal(key, dims, jnp.float32) * deviation * gain
    return jnp.minimum(jnp.maximum(array, -bound), bound).astype(kind)


def setup_inputs(seed: int = 0) -> dict:
    seeds = jax.random.split(jax.random.key(seed), 7)
    images = gaussian(seeds[0], (EXPOS, ROWS, COLS), 1.0, 6.0, ((0, 8), (1, 4)))
    psf_taps = jnp.clip(0.019897461 + 0.17932129 * jax.random.uniform(seeds[1], (EXPOS, 2, KTAPS), jnp.float32) ** shard_levels(seeds[1], (EXPOS, 2, KTAPS), ((0, 8),), -0.2, 0.2), 0.019897461, 0.19921875).astype(jnp.bfloat16)
    exposure_weights = jnp.clip(jnp.exp(math.log(8.0) - 2.7725887 * jax.random.uniform(seeds[2], (EXPOS,), jnp.float32) ** shard_levels(seeds[2], (EXPOS,), ((0, 8),), -0.2, 0.2)), 0.5, 8.0)
    dest_patch = draw_dest_patch(jax.random.fold_in(seeds[6], 71), 0)
    dest_cell = draw_dest_cell(jax.random.fold_in(seeds[6], 71), 0)
    shift_class = touch_ends(jax.random.randint(seeds[5], (EXPOS, 2, ROWS // TILE, COLS // TILE), 0, SHIFTS), jax.random.fold_in(seeds[5], 1), 0, SHIFTS - 1).astype(jnp.int32)
    return {"images": images, "psf_taps": psf_taps, "exposure_weights": exposure_weights, "dest_patch": dest_patch, "dest_cell": dest_cell, "shift_class": shift_class}


def lanczos_table(size, classes):
    out_pos = jnp.arange(size, dtype=jnp.float32)[None, :, None]
    src_pos = jnp.arange(size + 6, dtype=jnp.float32)[None, None, :] - 3.0
    frac = jnp.arange(classes, dtype=jnp.float32)[:, None, None] / classes
    dist = src_pos - out_pos - frac
    kernel = jnp.where(jnp.abs(dist) < 3.0, jnp.sinc(dist) * jnp.sinc(dist / 3.0), 0.0)
    kernel = kernel / jnp.sum(kernel, axis=2, keepdims=True)
    return kernel.astype(jnp.bfloat16)


def tile_windows(framed, tile, band, cols):
    padded = jnp.pad(framed, ((0, tile - 6), (3, tile - 3)))
    count_y = band // tile
    count_x = cols // tile
    width = cols + tile
    rmain = padded[:band].reshape(count_y, tile, width)
    rtail = padded[tile:tile + band].reshape(count_y, tile, width)[:, :6]
    rowwin = jnp.concatenate([rmain, rtail], axis=1)
    cmain = rowwin[:, :, :cols].reshape(count_y, tile + 6, count_x, tile)
    ctail = rowwin[:, :, tile:tile + cols].reshape(count_y, tile + 6, count_x, tile)[..., :6]
    return jnp.concatenate([cmain, ctail], axis=3)


def reference(images, psf_taps, exposure_weights, dest_patch, dest_cell, shift_class):
    table = lanczos_table(TILE, SHIFTS).astype(jnp.float32)
    reach = KTAPS // 2

    def one(carry, inputs):
        total, cover = carry
        image, taps, weight, patch, cell, classes = inputs
        taps = taps.astype(jnp.float32)
        raw = jnp.pad(image.astype(jnp.float32), ((0, 0), (reach, reach)))
        colpassed = jnp.zeros((ROWS, COLS), jnp.float32)
        for b in range(KTAPS):
            colpassed = colpassed + taps[1, b] * raw[:, b:b + COLS]
        colpassed = jnp.pad(colpassed.astype(jnp.bfloat16).astype(jnp.float32), ((reach, reach), (0, 0)))
        matched = jnp.zeros((ROWS, COLS), jnp.float32)
        for a in range(KTAPS):
            matched = matched + taps[0, a] * colpassed[a:a + ROWS]
        matched = matched.astype(jnp.bfloat16)
        framed = jnp.pad(matched, ((3, 3), (0, 0)))
        tiles = tile_windows(framed, TILE, ROWS, COLS).astype(jnp.float32)
        along_cols = table[classes[1]]
        half = jnp.einsum('yrxj,yxij->yxri', tiles, along_cols).astype(jnp.bfloat16).astype(jnp.float32)
        along_rows = table[classes[0]]
        warped = jnp.einsum('yxor,yxri->yxoi', along_rows, half).astype(jnp.bfloat16).astype(jnp.float32)
        where_to = jnp.where(patch >= 0, patch * CELLS + cell, PATCHES * CELLS).reshape(-1).astype(jnp.int32)
        total = total.at[where_to].add(weight * warped.reshape(-1, TILE, TILE), mode="drop")
        cover = cover.at[where_to].add(jnp.full(where_to.shape, weight, jnp.float32), mode="drop")
        return (total, cover), None

    start = (jnp.zeros((PATCHES * CELLS, TILE, TILE), jnp.float32), jnp.zeros((PATCHES * CELLS,), jnp.float32))
    (total, cover), unused = lax.scan(one, start, (images, psf_taps, exposure_weights, dest_patch, dest_cell, shift_class))
    coadd = total / jnp.maximum(cover, 1.0)[:, None, None]
    return coadd.reshape(PATCHES, CELLS, TILE, TILE), cover.reshape(PATCHES, CELLS)
```

```python
import functools

import jax
import jax.numpy as jnp
import ml_dtypes
import numpy as np
from jax import lax
from jax.experimental import pallas as pl
from jax.experimental.pallas import tpu as pltpu
from jax.sharding import PartitionSpec as P

TILE = 128
KTAPS = 13
SHIFTS = 8
CELLS = 64
CAP = 16
PCELLS = 8
HALO = 16
BLOCK = 256
CORES = 2
WINDOW = 160
CHUNK = 2
MESH = pl.DeviceIdType.MESH


def padded_2(cells, sides, width):
    for axis, dim in sides:
        count = lax.axis_size(axis)
        ends = count - 1
        head = lax.slice_in_dim(cells, 0, width, axis=dim)
        tail = lax.slice_in_dim(cells, cells.shape[dim] - width, cells.shape[dim], axis=dim)
        cells = jnp.concatenate(
            [
                lax.ppermute(tail, axis, [(i, (i + 1) % count) for i in range(ends)]),
                cells,
                lax.ppermute(head, axis, [((i + 1) % count, i) for i in range(ends)]),
            ],
            axis=dim,
        )
    return cells


def passed_along(x, axis, by):
    size = lax.axis_size(axis)
    pairs = [(i, i + by) for i in range(size) if 0 <= i + by < size]
    return lax.ppermute(x, axis, pairs)


def lanczos_table(size, classes):
    out_pos = jnp.arange(size, dtype=jnp.float32)[None, :, None]
    src_pos = jnp.arange(size + 6, dtype=jnp.float32)[None, None, :] - 3.0
    frac = jnp.arange(classes, dtype=jnp.float32)[:, None, None] / classes
    dist = src_pos - out_pos - frac
    kernel = jnp.where(jnp.abs(dist) < 3.0, jnp.sinc(dist) * jnp.sinc(dist / 3.0), 0.0)
    kernel = kernel / jnp.sum(kernel, axis=2, keepdims=True)
    return kernel.astype(jnp.bfloat16)


def column_pass(rows, taps):
    count, height, cols = rows.shape
    reach = KTAPS // 2
    blocks = cols // TILE
    padded = jnp.pad(rows, ((0, 0), (0, 0), (reach, TILE - reach)))
    main = padded[:, :, :cols].reshape(count, height, blocks, TILE)
    tail = padded[:, :, TILE : TILE + cols].reshape(count, height, blocks, TILE)[..., : 2 * reach]
    windows = jnp.concatenate([main, tail], axis=3)
    offset = jnp.arange(TILE + 2 * reach)[:, None] - jnp.arange(TILE)[None, :]
    marks = (offset[None] == jnp.arange(KTAPS)[:, None, None]).astype(jnp.float32)
    toeplitz = jnp.einsum("eb,bji->eji", taps.astype(jnp.float32), marks).astype(jnp.bfloat16)
    result = jnp.einsum("enxj,eji->enxi", windows, toeplitz, preferred_element_type=jnp.float32)
    return result.reshape(count, height, cols).astype(jnp.bfloat16)


def row_pass(colpassed, taps, out_rows):
    offset = jnp.arange(out_rows + KTAPS - 1)[None, :] - jnp.arange(out_rows)[:, None]
    marks = (offset[None] == jnp.arange(KTAPS)[:, None, None]).astype(jnp.float32)
    toeplitz = jnp.einsum("eb,bor->eor", taps.astype(jnp.float32), marks).astype(jnp.bfloat16)
    return jnp.einsum("eor,erc->eoc", toeplitz, colpassed, preferred_element_type=jnp.float32)


def tile_windows(framed):
    count, height, cols = framed.shape
    band = height - 6
    padded = jnp.pad(framed, ((0, 0), (0, TILE - 6), (3, TILE - 3)))
    count_y = band // TILE
    count_x = cols // TILE
    width = cols + TILE
    rmain = padded[:, :band].reshape(count, count_y, TILE, width)
    rtail = padded[:, TILE : TILE + band].reshape(count, count_y, TILE, width)[:, :, :6]
    rowwin = jnp.concatenate([rmain, rtail], axis=2)
    cmain = rowwin[..., :cols].reshape(count, count_y, TILE + 6, count_x, TILE)
    ctail = rowwin[..., TILE : TILE + cols].reshape(count, count_y, TILE + 6, count_x, TILE)[
        ..., :6
    ]
    return jnp.concatenate([cmain, ctail], axis=4)


def pick_table(classes, table):
    marks = (classes[..., None] == jnp.arange(SHIFTS, dtype=classes.dtype)).astype(jnp.bfloat16)
    flat = table.reshape(SHIFTS, -1)
    chosen = jnp.dot(marks.reshape(-1, SHIFTS), flat, preferred_element_type=jnp.float32)
    return chosen.astype(jnp.bfloat16).reshape(classes.shape + table.shape[1:])


def general(images, psf_taps, exposure_weights, dest_patch, dest_cell, shift_class):
    count = images.shape[0]
    band = images.shape[1]
    cols = images.shape[2]
    owners = lax.axis_size("patch")
    table = lanczos_table(TILE, SHIFTS)
    reach = KTAPS // 2
    raw = padded_2(images, (("patch", 1),), reach)
    colpassed = column_pass(raw, psf_taps[:, 1])
    matched = row_pass(colpassed, psf_taps[:, 0], band).astype(jnp.bfloat16)
    framed = padded_2(matched, (("patch", 1),), 3)
    tiles = tile_windows(framed)
    along_cols = pick_table(shift_class[:, 1], table)
    half = jnp.einsum(
        "eyrxj,eyxij->eyxri", tiles, along_cols, preferred_element_type=jnp.float32
    ).astype(jnp.bfloat16)
    count_y = band // TILE
    count_x = cols // TILE
    per_expo = count_y * count_x
    patch_flat = dest_patch.reshape(count, per_expo)
    hits = (patch_flat[..., None] == jnp.arange(owners, dtype=jnp.int32)).astype(jnp.int32)
    rank = jnp.sum(jnp.cumsum(hits, axis=1) * hits, axis=2) - 1
    expo_index = jnp.arange(count, dtype=jnp.int32)[:, None]
    cell_values = dest_cell.reshape(count, per_expo).astype(jnp.float32) + 1.0
    along_rows = pick_table(shift_class[:, 0], table)
    warped = jnp.einsum(
        "eyxor,eyxri->eyxoi", along_rows, half, preferred_element_type=jnp.float32
    ).astype(jnp.bfloat16)
    content = warped.reshape((count * per_expo, TILE, TILE))
    extra = cell_values[..., None]
    width = extra.shape[-1]
    extra = extra.reshape(count * per_expo, width)
    item_shape = content.shape[1:]
    flat_content = content.reshape(count * per_expo, -1)
    cell_numbers = (jnp.arange(CELLS) + 1).astype(jnp.bfloat16)
    state = (jnp.zeros((CELLS, TILE * TILE), jnp.float32), jnp.zeros((CELLS,), jnp.float32))
    position = lax.axis_index("patch")
    span = min(4, owners - 1)
    for offset in range(-span, span + 1):
        slot = jnp.where(
            patch_flat == position + offset, expo_index * CAP + rank, count * CAP
        ).reshape(-1)
        slots = count * CAP
        picks = jnp.arange(slots, dtype=jnp.int32)[:, None] == slot[None, :]
        pack_placed = jnp.dot(
            picks.astype(jnp.bfloat16), flat_content, preferred_element_type=jnp.float32
        )
        pack_buffer = pack_placed.astype(jnp.bfloat16).reshape((slots,) + item_shape)
        pack_labels = jnp.dot(
            picks.astype(jnp.float32), extra, precision=lax.Precision.HIGHEST
        ).astype(jnp.bfloat16)
        buffer = pack_buffer
        labels = pack_labels
        buffer = buffer.reshape((1, count, CAP) + item_shape)
        labels = labels.reshape(1, count, CAP, width)
        if offset != 0:
            buffer, labels = passed_along((buffer, labels), "patch", offset)
        accumulate_total, accumulate_cover = state
        chosen = (cell_numbers[:, None] == labels[:, 0, :, 0]).astype(jnp.bfloat16)
        placed = jnp.dot(
            chosen, buffer[:, 0].reshape(-1, TILE * TILE), preferred_element_type=jnp.float32
        )
        accumulate_total = accumulate_total + exposure_weights[0] * placed
        accumulate_cover = accumulate_cover + exposure_weights[0] * jnp.sum(
            chosen.astype(jnp.float32), axis=1
        )
        state = (accumulate_total, accumulate_cover)
    total, cover = state
    total_sum, cover_sum = (
        lax.psum_scatter(
            total.reshape(1, CELLS, TILE, TILE), "visit", scatter_dimension=1, tiled=True
        ),
        lax.psum_scatter(cover.reshape(1, CELLS), "visit", scatter_dimension=1, tiled=True),
    )
    coadd = total_sum / jnp.maximum(cover_sum, 1.0)[:, :, None, None]
    return (coadd, cover_sum)


def lanczos_windows():
    out_pos = np.arange(TILE, dtype=np.float64)[None, :, None]
    src_pos = np.arange(TILE + 6, dtype=np.float64)[None, None, :] - 3.0
    dist = src_pos - out_pos - np.arange(SHIFTS, dtype=np.float64)[:, None, None] / SHIFTS
    kernel = np.where(np.abs(dist) < 3.0, np.sinc(dist) * np.sinc(dist / 3.0), 0.0)
    kernel = kernel / np.sum(kernel, axis=2, keepdims=True)
    by_cols = np.zeros((SHIFTS, 3 * TILE, TILE), np.float64)
    by_cols[:, TILE - 3 : 2 * TILE + 3] = kernel.transpose(0, 2, 1)
    by_rows = np.zeros((SHIFTS, TILE, WINDOW), np.float64)
    by_rows[:, :, HALO - 3 : HALO + TILE + 3] = kernel
    return by_cols.astype(ml_dtypes.bfloat16), by_rows.astype(ml_dtypes.bfloat16)


def warp_kernel(
    taps, weight, patch, cell, classes, image, above, below, by_cols, by_rows,
    tiles, marks, framed, matched, source,
):
    band, cols = image.shape
    height = band + 2 * HALO
    count_x = cols // TILE
    slots = tiles.shape[0]
    reach = KTAPS // 2
    position = lax.axis_index("patch")
    last = lax.axis_size("patch") - 1

    def empty(i, carry):
        source[0, i] = 0
        source[1, i] = -1
        return carry

    lax.fori_loop(0, slots, empty, 0)

    def place(i, carry):
        @pl.when(patch[i] >= 0)
        def _():
            row = cell[i] // PCELLS
            slot = (patch[i] * CORES + row % CORES) * PCELLS + cell[i] % PCELLS
            source[0, slot] = i
            source[1, slot] = row // CORES

        return carry

    lax.fori_loop(0, slots, place, 0)

    framed[:, 0:TILE] = jnp.zeros((height, TILE), jnp.bfloat16)
    framed[:, TILE + cols :] = jnp.zeros((height, TILE), jnp.bfloat16)
    matched[:, 0:TILE] = jnp.zeros((height, TILE), jnp.bfloat16)
    matched[:, TILE + cols :] = jnp.zeros((height, TILE), jnp.bfloat16)
    framed[0:HALO, TILE : TILE + cols] = above[...]
    framed[HALO : HALO + band, TILE : TILE + cols] = image[...]
    framed[HALO + band :, TILE : TILE + cols] = below[...]

    shape = (BLOCK + 2 * TILE, BLOCK)
    lag = (
        lax.broadcasted_iota(jnp.int32, shape, 0)
        - lax.broadcasted_iota(jnp.int32, shape, 1)
        - (TILE - reach)
    )
    along = jnp.zeros(shape, jnp.float32)
    for b in range(KTAPS):
        along = jnp.where(lag == b, taps[KTAPS + b], along)
    along = along.astype(jnp.bfloat16)
    shape = (height, height)
    out_row = lax.broadcasted_iota(jnp.int32, shape, 0)
    lag = lax.broadcasted_iota(jnp.int32, shape, 1) - out_row + reach
    down = jnp.zeros(shape, jnp.float32)
    for a in range(KTAPS):
        down = jnp.where(lag == a, taps[a], down)
    low = jnp.where(position == 0, HALO, 0)
    high = jnp.where(position == last, HALO + band, height)
    down = jnp.where((out_row >= low) & (out_row < high), down, 0.0).astype(jnp.bfloat16)

    def match(i, carry):
        start = pl.multiple_of(i * BLOCK, BLOCK)
        wide = framed[:, pl.ds(start, BLOCK + 2 * TILE)]
        passed = jnp.dot(wide, along, preferred_element_type=jnp.float32).astype(jnp.bfloat16)
        result = jnp.dot(down, passed, preferred_element_type=jnp.float32).astype(jnp.bfloat16)
        matched[:, pl.ds(pl.multiple_of(start + TILE, TILE), BLOCK)] = result
        return carry

    lax.fori_loop(0, cols // BLOCK, match, 0, unroll=2)

    def warp(slot, carry):
        tile = source[0, slot]
        top = pl.multiple_of(tile // count_x * TILE, TILE)
        left = pl.multiple_of(tile % count_x * TILE, TILE)
        window = matched[pl.ds(top, WINDOW), pl.ds(left, 3 * TILE)]
        half = jnp.dot(
            window, by_cols[classes[slots + tile]], preferred_element_type=jnp.float32
        ).astype(jnp.bfloat16)
        warped = jnp.dot(by_rows[classes[tile]], half, preferred_element_type=jnp.float32)
        tiles[slot] = warped.astype(jnp.bfloat16)
        return carry

    lax.fori_loop(0, slots, warp, 0, unroll=4)

    row_of = lax.broadcasted_iota(jnp.int32, (PCELLS, TILE), 0)
    lane_of = lax.broadcasted_iota(jnp.int32, (PCELLS, TILE), 1)

    def mark(owner, carry):
        held = jnp.zeros((PCELLS, TILE), jnp.float32)
        for j in range(PCELLS):
            here = (row_of == source[1, owner * PCELLS + j]) & (lane_of == j)
            held = jnp.where(here, weight[0], held)
        marks[owner] = held
        return carry

    lax.fori_loop(0, slots // PCELLS, mark, 0)


def exchange_kernel(
    tiles, marks, coadd, cover, got, got_marks, factor, sums, came,
    tile_out, tile_in, mark_out, mark_in, sum_out, sum_in, own_sem,
):
    owners = tiles.shape[0]
    layers = sums.shape[0]
    chunks = PCELLS // CHUNK
    visit = lax.axis_index("visit")
    patch = lax.axis_index("patch")
    layer = visit // CORES
    core = visit % CORES
    me = patch * CORES + core

    def beside(k):
        other = lax.rem(me + k, owners)
        return other, (layer * CORES + other % CORES, other // CORES)

    def along(k):
        other = lax.rem(layer + k, layers)
        return other, (other * CORES + core, patch)

    barrier = pltpu.get_barrier_semaphore()
    for k in range(1, owners):
        pl.semaphore_signal(barrier, inc=1, device_id=beside(k)[1], device_id_type=MESH)
    for k in range(1, layers):
        pl.semaphore_signal(barrier, inc=1, device_id=along(k)[1], device_id_type=MESH)
    pl.semaphore_wait(barrier, owners + layers - 2)

    def mark_copy(k):
        other, device = beside(k)
        return pltpu.make_async_remote_copy(
            src_ref=marks.at[other], dst_ref=got_marks.at[me],
            send_sem=mark_out.at[k], recv_sem=mark_in.at[k],
            device_id=device, device_id_type=MESH,
        )

    def tile_copy(g, k):
        other, device = beside(k)
        part = pl.ds(g * CHUNK, CHUNK)
        return pltpu.make_async_remote_copy(
            src_ref=tiles.at[other, part], dst_ref=got.at[me, part],
            send_sem=tile_out.at[g, k], recv_sem=tile_in.at[g, k],
            device_id=device, device_id_type=MESH,
        )

    def sum_copy(g, k):
        other, device = along(k)
        part = pl.ds(g * CHUNK, CHUNK)
        return pltpu.make_async_remote_copy(
            src_ref=sums.at[other, part], dst_ref=came.at[layer, part],
            send_sem=sum_out.at[g, k], recv_sem=sum_in.at[g, k],
            device_id=device, device_id_type=MESH,
        )

    for k in range(1, owners):
        mark_copy(k).start()
    for g in range(chunks):
        for k in range(1, owners):
            tile_copy(g, k).start()
    own = pltpu.make_async_copy(tiles.at[me], got.at[me], own_sem)
    own.start()
    got_marks[me] = marks[me]
    for k in range(1, owners):
        mark_copy(k).wait_recv()
    lane_of = lax.broadcasted_iota(jnp.int32, (PCELLS, TILE), 1)
    for i in range(owners):
        held = got_marks[i]
        for j in range(PCELLS):
            picked = jnp.sum(jnp.where(lane_of == j, held, 0.0), axis=1, keepdims=True)
            factor[i, j] = jnp.broadcast_to(picked, (PCELLS, TILE))
    own.wait()

    def terms(row):
        bands = [b for b in (row - 1, row, row + 1) if 0 <= b < owners // CORES]
        return [b * CORES + e for b in bands for e in range(CORES)]

    for g in range(chunks):
        for k in range(1, owners):
            tile_copy(g, k).wait_recv()
        for j in range(g * CHUNK, (g + 1) * CHUNK):
            gain = {
                (i, row): factor[i, j, row : row + 1, :]
                for row in range(layers)
                for i in terms(row)
            }
            for row in range(layers):
                seen = functools.reduce(lambda a, b: a + b, [gain[i, row] for i in terms(row)])
                sums[row, j, TILE:, :] = jnp.broadcast_to(seen, (PCELLS, TILE))

            def add(n, carry, j=j, gain=gain):
                rows = pl.ds(pl.multiple_of(n * 16, 16), 16)
                held = [got[i, j, rows, :].astype(jnp.float32) for i in range(owners)]
                for row in range(layers):
                    parts = [gain[i, row] * held[i] for i in terms(row)]
                    sums[row, j, rows, :] = functools.reduce(lambda a, b: a + b, parts)
                return carry

            lax.fori_loop(0, TILE // 16, add, 0)
        for k in range(1, layers):
            sum_copy(g, k).start()
    for g in range(chunks):
        for k in range(1, layers):
            sum_copy(g, k).wait_recv()
        for j in range(g * CHUNK, (g + 1) * CHUNK):
            whole = sums[layer, j]
            for k in range(1, layers):
                whole = whole + came[lax.rem(layer + k, layers), j]
            weight = whole[TILE : TILE + 1, :]
            coadd[j] = whole[:TILE] / jnp.maximum(weight, 1.0)
            cover[j : j + 1, :] = weight
    for k in range(1, owners):
        mark_copy(k).wait_send()
        for g in range(chunks):
            tile_copy(g, k).wait_send()
    for k in range(1, layers):
        for g in range(chunks):
            sum_copy(g, k).wait_send()


def whole_rows(images, psf_taps, exposure_weights, dest_patch, dest_cell, shift_class):
    band, cols = images.shape[1:]
    bands = lax.axis_size("patch")
    layers = lax.axis_size("visit") // CORES
    owners = bands * CORES
    slots = owners * PCELLS
    image = images[0]
    above = lax.ppermute(image[band - HALO :], "patch", [(i, i + 1) for i in range(bands - 1)])
    below = lax.ppermute(image[:HALO], "patch", [(i + 1, i) for i in range(bands - 1)])
    by_cols, by_rows = lanczos_windows()
    scalars = pl.BlockSpec(memory_space=pltpu.SMEM)
    vector = pl.BlockSpec(memory_space=pltpu.VMEM)
    height = band + 2 * HALO
    wide = cols + 2 * TILE
    tiles, marks = pl.pallas_call(
        warp_kernel,
        out_shape=(
            jax.ShapeDtypeStruct((slots, TILE, TILE), jnp.bfloat16),
            jax.ShapeDtypeStruct((owners, PCELLS, TILE), jnp.float32),
        ),
        in_specs=[scalars] * 5 + [vector] * 5,
        out_specs=(vector, vector),
        scratch_shapes=[
            pltpu.VMEM((height, wide), jnp.bfloat16),
            pltpu.VMEM((height, wide), jnp.bfloat16),
            pltpu.SMEM((2, slots), jnp.int32),
        ],
        compiler_params=pltpu.CompilerParams(vmem_limit_bytes=40 * 2**20),
        cost_estimate=pl.CostEstimate(
            flops=3 * 10**9, bytes_accessed=6 * 2**20, transcendentals=0
        ),
        name="match_and_warp",
    )(
        psf_taps.astype(jnp.float32).reshape(-1),
        exposure_weights,
        dest_patch.reshape(-1),
        dest_cell.reshape(-1),
        shift_class.reshape(-1),
        image,
        above,
        below,
        jnp.asarray(by_cols),
        jnp.asarray(by_rows),
    )
    chunks = PCELLS // CHUNK
    dma = pltpu.SemaphoreType.DMA
    coadd, cover = pl.pallas_call(
        exchange_kernel,
        out_shape=(
            jax.ShapeDtypeStruct((PCELLS, TILE, TILE), jnp.float32),
            jax.ShapeDtypeStruct((PCELLS, TILE), jnp.float32),
        ),
        in_specs=[vector, vector],
        out_specs=(vector, vector),
        scratch_shapes=[
            pltpu.VMEM((owners, PCELLS, TILE, TILE), jnp.bfloat16),
            pltpu.VMEM((owners, PCELLS, TILE), jnp.float32),
            pltpu.VMEM((owners, PCELLS, PCELLS, TILE), jnp.float32),
            pltpu.VMEM((layers, PCELLS, TILE + PCELLS, TILE), jnp.float32),
            pltpu.VMEM((layers, PCELLS, TILE + PCELLS, TILE), jnp.float32),
            dma((chunks, owners)),
            dma((chunks, owners)),
            dma((owners,)),
            dma((owners,)),
            dma((chunks, layers)),
            dma((chunks, layers)),
            dma,
        ],
        compiler_params=pltpu.CompilerParams(
            collective_id=0, has_side_effects=True, vmem_limit_bytes=40 * 2**20
        ),
        cost_estimate=pl.CostEstimate(
            flops=10**8, bytes_accessed=6 * 2**20, transcendentals=0
        ),
        name="exchange_and_sum",
    )(tiles.reshape(owners, PCELLS, TILE, TILE), marks)
    return coadd[None], cover[:, 0][None]


def local(images, psf_taps, exposure_weights, dest_patch, dest_cell, shift_class):
    count, band, cols = images.shape
    owners = lax.axis_size("patch")
    visits = lax.axis_size("visit")
    row_of_patches = (
        count == 1
        and band == CORES * TILE
        and owners * band == PCELLS * TILE
        and cols == owners * PCELLS * TILE
        and visits == PCELLS
    )
    plan = whole_rows if row_of_patches else general
    return plan(images, psf_taps, exposure_weights, dest_patch, dest_cell, shift_class)


def solution(mesh):
    placed = (
        P("visit", "patch", None),
        P("visit", None, None),
        P("visit"),
        P("visit", "patch", None),
        P("visit", "patch", None),
        P("visit", None, "patch", None),
    )
    return jax.shard_map(
        local,
        mesh=mesh,
        in_specs=placed,
        out_specs=(P("patch", "visit", None, None), P("patch", "visit")),
        check_vma=False,
    )
```

```python
import functools

import jax
import jax.numpy as jnp
import ml_dtypes
import numpy as np
from jax import lax
from jax.experimental import pallas as pl
from jax.experimental.pallas import tpu as pltpu
from jax.sharding import PartitionSpec as P

TILE = 128
KTAPS = 13
SHIFTS = 8
CELLS = 64
CAP = 16
PCELLS = 8
HALO = 16
BLOCK = 256
CORES = 2
WINDOW = 144
EDGE = 3
CHUNK = 2
MESH = pl.DeviceIdType.MESH


def padded_2(cells, sides, width):
    for axis, dim in sides:
        count = lax.axis_size(axis)
        ends = count - 1
        head = lax.slice_in_dim(cells, 0, width, axis=dim)
        tail = lax.slice_in_dim(cells, cells.shape[dim] - width, cells.shape[dim], axis=dim)
        cells = jnp.concatenate(
            [
                lax.ppermute(tail, axis, [(i, (i + 1) % count) for i in range(ends)]),
                cells,
                lax.ppermute(head, axis, [((i + 1) % count, i) for i in range(ends)]),
            ],
            axis=dim,
        )
    return cells


def passed_along(x, axis, by):
    size = lax.axis_size(axis)
    pairs = [(i, i + by) for i in range(size) if 0 <= i + by < size]
    return lax.ppermute(x, axis, pairs)


def lanczos_table(size, classes):
    out_pos = jnp.arange(size, dtype=jnp.float32)[None, :, None]
    src_pos = jnp.arange(size + 6, dtype=jnp.float32)[None, None, :] - 3.0
    frac = jnp.arange(classes, dtype=jnp.float32)[:, None, None] / classes
    dist = src_pos - out_pos - frac
    kernel = jnp.where(jnp.abs(dist) < 3.0, jnp.sinc(dist) * jnp.sinc(dist / 3.0), 0.0)
    kernel = kernel / jnp.sum(kernel, axis=2, keepdims=True)
    return kernel.astype(jnp.bfloat16)


def column_pass(rows, taps):
    count, height, cols = rows.shape
    reach = KTAPS // 2
    blocks = cols // TILE
    padded = jnp.pad(rows, ((0, 0), (0, 0), (reach, TILE - reach)))
    main = padded[:, :, :cols].reshape(count, height, blocks, TILE)
    tail = padded[:, :, TILE : TILE + cols].reshape(count, height, blocks, TILE)[..., : 2 * reach]
    windows = jnp.concatenate([main, tail], axis=3)
    offset = jnp.arange(TILE + 2 * reach)[:, None] - jnp.arange(TILE)[None, :]
    marks = (offset[None] == jnp.arange(KTAPS)[:, None, None]).astype(jnp.float32)
    toeplitz = jnp.einsum("eb,bji->eji", taps.astype(jnp.float32), marks).astype(jnp.bfloat16)
    result = jnp.einsum("enxj,eji->enxi", windows, toeplitz, preferred_element_type=jnp.float32)
    return result.reshape(count, height, cols).astype(jnp.bfloat16)


def row_pass(colpassed, taps, out_rows):
    offset = jnp.arange(out_rows + KTAPS - 1)[None, :] - jnp.arange(out_rows)[:, None]
    marks = (offset[None] == jnp.arange(KTAPS)[:, None, None]).astype(jnp.float32)
    toeplitz = jnp.einsum("eb,bor->eor", taps.astype(jnp.float32), marks).astype(jnp.bfloat16)
    return jnp.einsum("eor,erc->eoc", toeplitz, colpassed, preferred_element_type=jnp.float32)


def tile_windows(framed):
    count, height, cols = framed.shape
    band = height - 6
    padded = jnp.pad(framed, ((0, 0), (0, TILE - 6), (3, TILE - 3)))
    count_y = band // TILE
    count_x = cols // TILE
    width = cols + TILE
    rmain = padded[:, :band].reshape(count, count_y, TILE, width)
    rtail = padded[:, TILE : TILE + band].reshape(count, count_y, TILE, width)[:, :, :6]
    rowwin = jnp.concatenate([rmain, rtail], axis=2)
    cmain = rowwin[..., :cols].reshape(count, count_y, TILE + 6, count_x, TILE)
    ctail = rowwin[..., TILE : TILE + cols].reshape(count, count_y, TILE + 6, count_x, TILE)[
        ..., :6
    ]
    return jnp.concatenate([cmain, ctail], axis=4)


def pick_table(classes, table):
    marks = (classes[..., None] == jnp.arange(SHIFTS, dtype=classes.dtype)).astype(jnp.bfloat16)
    flat = table.reshape(SHIFTS, -1)
    chosen = jnp.dot(marks.reshape(-1, SHIFTS), flat, preferred_element_type=jnp.float32)
    return chosen.astype(jnp.bfloat16).reshape(classes.shape + table.shape[1:])


def general(images, psf_taps, exposure_weights, dest_patch, dest_cell, shift_class):
    count = images.shape[0]
    band = images.shape[1]
    cols = images.shape[2]
    owners = lax.axis_size("patch")
    table = lanczos_table(TILE, SHIFTS)
    reach = KTAPS // 2
    raw = padded_2(images, (("patch", 1),), reach)
    colpassed = column_pass(raw, psf_taps[:, 1])
    matched = row_pass(colpassed, psf_taps[:, 0], band).astype(jnp.bfloat16)
    framed = padded_2(matched, (("patch", 1),), 3)
    tiles = tile_windows(framed)
    along_cols = pick_table(shift_class[:, 1], table)
    half = jnp.einsum(
        "eyrxj,eyxij->eyxri", tiles, along_cols, preferred_element_type=jnp.float32
    ).astype(jnp.bfloat16)
    count_y = band // TILE
    count_x = cols // TILE
    per_expo = count_y * count_x
    patch_flat = dest_patch.reshape(count, per_expo)
    hits = (patch_flat[..., None] == jnp.arange(owners, dtype=jnp.int32)).astype(jnp.int32)
    rank = jnp.sum(jnp.cumsum(hits, axis=1) * hits, axis=2) - 1
    expo_index = jnp.arange(count, dtype=jnp.int32)[:, None]
    cell_values = dest_cell.reshape(count, per_expo).astype(jnp.float32) + 1.0
    along_rows = pick_table(shift_class[:, 0], table)
    warped = jnp.einsum(
        "eyxor,eyxri->eyxoi", along_rows, half, preferred_element_type=jnp.float32
    ).astype(jnp.bfloat16)
    content = warped.reshape((count * per_expo, TILE, TILE))
    extra = cell_values[..., None]
    width = extra.shape[-1]
    extra = extra.reshape(count * per_expo, width)
    item_shape = content.shape[1:]
    flat_content = content.reshape(count * per_expo, -1)
    cell_numbers = (jnp.arange(CELLS) + 1).astype(jnp.bfloat16)
    state = (jnp.zeros((CELLS, TILE * TILE), jnp.float32), jnp.zeros((CELLS,), jnp.float32))
    position = lax.axis_index("patch")
    span = min(4, owners - 1)
    for offset in range(-span, span + 1):
        slot = jnp.where(
            patch_flat == position + offset, expo_index * CAP + rank, count * CAP
        ).reshape(-1)
        slots = count * CAP
        picks = jnp.arange(slots, dtype=jnp.int32)[:, None] == slot[None, :]
        pack_placed = jnp.dot(
            picks.astype(jnp.bfloat16), flat_content, preferred_element_type=jnp.float32
        )
        pack_buffer = pack_placed.astype(jnp.bfloat16).reshape((slots,) + item_shape)
        pack_labels = jnp.dot(
            picks.astype(jnp.float32), extra, precision=lax.Precision.HIGHEST
        ).astype(jnp.bfloat16)
        buffer = pack_buffer
        labels = pack_labels
        buffer = buffer.reshape((1, count, CAP) + item_shape)
        labels = labels.reshape(1, count, CAP, width)
        if offset != 0:
            buffer, labels = passed_along((buffer, labels), "patch", offset)
        accumulate_total, accumulate_cover = state
        chosen = (cell_numbers[:, None] == labels[:, 0, :, 0]).astype(jnp.bfloat16)
        placed = jnp.dot(
            chosen, buffer[:, 0].reshape(-1, TILE * TILE), preferred_element_type=jnp.float32
        )
        accumulate_total = accumulate_total + exposure_weights[0] * placed
        accumulate_cover = accumulate_cover + exposure_weights[0] * jnp.sum(
            chosen.astype(jnp.float32), axis=1
        )
        state = (accumulate_total, accumulate_cover)
    total, cover = state
    total_sum, cover_sum = (
        lax.psum_scatter(
            total.reshape(1, CELLS, TILE, TILE), "visit", scatter_dimension=1, tiled=True
        ),
        lax.psum_scatter(cover.reshape(1, CELLS), "visit", scatter_dimension=1, tiled=True),
    )
    coadd = total_sum / jnp.maximum(cover_sum, 1.0)[:, :, None, None]
    return (coadd, cover_sum)


def lanczos_windows():
    out_pos = np.arange(TILE, dtype=np.float64)[None, :, None]
    src_pos = np.arange(TILE + 6, dtype=np.float64)[None, None, :] - 3.0
    dist = src_pos - out_pos - np.arange(SHIFTS, dtype=np.float64)[:, None, None] / SHIFTS
    kernel = np.where(np.abs(dist) < 3.0, np.sinc(dist) * np.sinc(dist / 3.0), 0.0)
    kernel = kernel / np.sum(kernel, axis=2, keepdims=True)
    by_cols = np.zeros((SHIFTS, 2 * TILE, TILE), np.float64)
    by_cols[:, : TILE + 2 * EDGE] = kernel.transpose(0, 2, 1)
    by_rows = np.zeros((SHIFTS, TILE, WINDOW), np.float64)
    by_rows[:, :, : TILE + 2 * EDGE] = kernel
    return by_cols.astype(ml_dtypes.bfloat16), by_rows.astype(ml_dtypes.bfloat16)


def warp_kernel(
    patches, cells, classes, weight, taps, image, above, below, table_cols, table_rows,
    tiles, marks, framed, matched, by_cols, by_rows, source, sems,
):
    band, cols = image.shape[1:]
    count_x = cols // TILE
    height = band + 2 * HALO
    reach = KTAPS // 2
    slots = tiles.shape[0]
    patch = lax.axis_index("patch")
    last = lax.axis_size("patch") - 1

    framed[:, 0:TILE] = jnp.zeros((height, TILE), jnp.bfloat16)
    framed[:, TILE + cols :] = jnp.zeros((height, framed.shape[1] - TILE - cols), jnp.bfloat16)
    pieces = ((image.at[0], HALO, band), (above, 0, HALO), (below, HALO + band, HALO))
    loads = [
        pltpu.make_async_copy(ref, framed.at[pl.ds(top, rows), pl.ds(TILE, cols)], sems.at[i])
        for i, (ref, top, rows) in enumerate(pieces)
    ]
    load_cols = pltpu.make_async_copy(table_cols, by_cols, sems.at[3])
    load_rows = pltpu.make_async_copy(table_rows, by_rows, sems.at[4])
    for load in loads + [load_cols, load_rows]:
        load.start()

    def empty(i, carry):
        source[0, i] = 0
        source[1, i] = -1
        return carry

    lax.fori_loop(0, slots, empty, 0)

    def place(i, carry):
        y, x = i // count_x, i % count_x
        owner = patches[0, y, x]

        @pl.when(owner >= 0)
        def _():
            cell = cells[0, y, x]
            row = cell // PCELLS
            slot = (owner * CORES + row % CORES) * PCELLS + cell % PCELLS
            source[0, slot] = i
            source[1, slot] = row // CORES

        return carry

    lax.fori_loop(0, slots, place, 0)

    tap = taps[0].astype(jnp.float32)
    shape = (BLOCK + 2 * TILE, BLOCK)
    lag = (
        lax.broadcasted_iota(jnp.int32, shape, 0)
        - lax.broadcasted_iota(jnp.int32, shape, 1)
        - (TILE - reach - EDGE)
    )
    across = jnp.zeros(shape, jnp.float32)
    for b in range(KTAPS):
        across = jnp.where(lag == b, tap[1:2, b : b + 1], across)
    across = across.astype(jnp.bfloat16)
    shape = (matched.shape[0], height)
    frame_row = lax.broadcasted_iota(jnp.int32, shape, 0) + (HALO - EDGE)
    lag = lax.broadcasted_iota(jnp.int32, shape, 1) - frame_row + reach
    down = jnp.zeros(shape, jnp.float32)
    for a in range(KTAPS):
        down = jnp.where(lag == a, tap[0:1, a : a + 1], down)
    low = jnp.where(patch == 0, HALO, 0)
    high = jnp.where(patch == last, HALO + band, height)
    down = jnp.where((frame_row >= low) & (frame_row < high), down, 0.0).astype(jnp.bfloat16)

    for load in loads:
        load.wait()

    def match(i, carry):
        start = pl.multiple_of(i * BLOCK, BLOCK)
        wide = framed[:, pl.ds(start, BLOCK + 2 * TILE)]
        passed = jnp.dot(wide, across, preferred_element_type=jnp.float32).astype(jnp.bfloat16)
        result = jnp.dot(down, passed, preferred_element_type=jnp.float32).astype(jnp.bfloat16)
        matched[:, pl.ds(start, BLOCK)] = result
        return carry

    lax.fori_loop(0, cols // BLOCK, match, 0, unroll=4)
    wide = framed[:, cols : cols + 3 * TILE]
    passed = jnp.dot(
        wide, across[: 3 * TILE, :TILE], preferred_element_type=jnp.float32
    ).astype(jnp.bfloat16)
    result = jnp.dot(down, passed, preferred_element_type=jnp.float32)
    lane = lax.broadcasted_iota(jnp.int32, result.shape, 1)
    matched[:, cols:] = jnp.where(lane < EDGE, result, 0.0).astype(jnp.bfloat16)
    begin = matched[:, 0:TILE].astype(jnp.float32)
    matched[:, 0:TILE] = jnp.where(lane < EDGE, 0.0, begin).astype(jnp.bfloat16)
    load_cols.wait()
    load_rows.wait()

    def warp(n, carry):
        todo = [n * PCELLS + j for j in range(PCELLS)]
        places = [(source[0, t] // count_x, source[0, t] % count_x) for t in todo]
        halves = []
        for y, x in places:
            top = pl.multiple_of(y * TILE, TILE)
            left = pl.multiple_of(x * TILE, TILE)
            window = matched[pl.ds(top, WINDOW), pl.ds(left, 2 * TILE)]
            halves.append(
                jnp.dot(
                    window, by_cols[classes[0, 1, y, x]], preferred_element_type=jnp.float32
                ).astype(jnp.bfloat16)
            )
        warped = [
            jnp.dot(by_rows[classes[0, 0, y, x]], half, preferred_element_type=jnp.float32)
            for (y, x), half in zip(places, halves)
        ]
        for t, block in zip(todo, warped):
            tiles[t] = block.astype(jnp.bfloat16)
        return carry

    lax.fori_loop(0, slots // PCELLS, warp, 0)

    row_of = lax.broadcasted_iota(jnp.int32, (PCELLS, TILE), 0)
    lane_of = lax.broadcasted_iota(jnp.int32, (PCELLS, TILE), 1)

    def mark(owner, carry):
        held = jnp.zeros((PCELLS, TILE), jnp.float32)
        for j in range(PCELLS):
            here = (row_of == source[1, owner * PCELLS + j]) & (lane_of == j)
            held = jnp.where(here, weight[0], held)
        marks[owner] = held
        return carry

    lax.fori_loop(0, slots // PCELLS, mark, 0)


def exchange_kernel(
    tiles, marks, coadd, cover, got, got_marks, factor, sums, came,
    tile_out, tile_in, mark_out, mark_in, sum_out, sum_in, own_sem,
):
    owners = tiles.shape[0]
    layers = sums.shape[0]
    chunks = PCELLS // CHUNK
    visit = lax.axis_index("visit")
    patch = lax.axis_index("patch")
    layer = visit // CORES
    core = visit % CORES
    me = patch * CORES + core

    def beside(k):
        other = lax.rem(me + k, owners)
        return other, (layer * CORES + other % CORES, other // CORES)

    def along(k):
        other = lax.rem(layer + k, layers)
        return other, (other * CORES + core, patch)

    barrier = pltpu.get_barrier_semaphore()
    for k in range(1, owners):
        pl.semaphore_signal(barrier, inc=1, device_id=beside(k)[1], device_id_type=MESH)
    for k in range(1, layers):
        pl.semaphore_signal(barrier, inc=1, device_id=along(k)[1], device_id_type=MESH)
    pl.semaphore_wait(barrier, owners + layers - 2)

    def mark_copy(k):
        other, device = beside(k)
        return pltpu.make_async_remote_copy(
            src_ref=marks.at[other], dst_ref=got_marks.at[me],
            send_sem=mark_out.at[k], recv_sem=mark_in.at[k],
            device_id=device, device_id_type=MESH,
        )

    def tile_copy(g, k):
        other, device = beside(k)
        part = pl.ds(g * CHUNK, CHUNK)
        return pltpu.make_async_remote_copy(
            src_ref=tiles.at[other, part], dst_ref=got.at[me, part],
            send_sem=tile_out.at[g, k], recv_sem=tile_in.at[g, k],
            device_id=device, device_id_type=MESH,
        )

    def sum_copy(g, k):
        other, device = along(k)
        part = pl.ds(g * CHUNK, CHUNK)
        return pltpu.make_async_remote_copy(
            src_ref=sums.at[other, part], dst_ref=came.at[layer, part],
            send_sem=sum_out.at[g, k], recv_sem=sum_in.at[g, k],
            device_id=device, device_id_type=MESH,
        )

    for k in range(1, owners):
        mark_copy(k).start()
    for g in range(2):
        for k in range(1, owners):
            tile_copy(g, k).start()
    own = pltpu.make_async_copy(tiles.at[me], got.at[me], own_sem)
    own.start()
    got_marks[me] = marks[me]
    for k in range(1, owners):
        mark_copy(k).wait_recv()
    lane_of = lax.broadcasted_iota(jnp.int32, (PCELLS, TILE), 1)
    for i in range(owners):
        held = got_marks[i]
        for j in range(PCELLS):
            picked = jnp.sum(jnp.where(lane_of == j, held, 0.0), axis=1, keepdims=True)
            factor[i, j] = jnp.broadcast_to(picked, (PCELLS, TILE))
    own.wait()

    def terms(row):
        bands = [b for b in (row - 1, row, row + 1) if 0 <= b < owners // CORES]
        return [b * CORES + e for b in bands for e in range(CORES)]

    for g in range(chunks):
        for k in range(1, owners):
            tile_copy(g, k).wait_recv()
        if g + 2 < chunks:
            for k in range(1, owners):
                tile_copy(g + 2, k).start()
        for j in range(g * CHUNK, (g + 1) * CHUNK):
            gain = {
                (i, row): factor[i, j, row : row + 1, :]
                for row in range(layers)
                for i in terms(row)
            }
            for row in range(layers):
                seen = functools.reduce(lambda a, b: a + b, [gain[i, row] for i in terms(row)])
                sums[row, j, TILE:, :] = jnp.broadcast_to(seen, (PCELLS, TILE))

            def add(n, carry, j=j, gain=gain):
                rows = pl.ds(pl.multiple_of(n * 16, 16), 16)
                held = [got[i, j, rows, :].astype(jnp.float32) for i in range(owners)]
                for row in range(layers):
                    parts = [gain[i, row] * held[i] for i in terms(row)]
                    sums[row, j, rows, :] = functools.reduce(lambda a, b: a + b, parts)
                return carry

            lax.fori_loop(0, TILE // 16, add, 0)
        for k in range(1, layers):
            sum_copy(g, k).start()
    for g in range(chunks):
        for k in range(1, layers):
            sum_copy(g, k).wait_recv()
        for j in range(g * CHUNK, (g + 1) * CHUNK):
            whole = sums[layer, j]
            for k in range(1, layers):
                whole = whole + came[lax.rem(layer + k, layers), j]
            weight = whole[TILE : TILE + 1, :]
            coadd[j] = whole[:TILE] / jnp.maximum(weight, 1.0)
            cover[j : j + 1, :] = weight
    for k in range(1, owners):
        mark_copy(k).wait_send()
        for g in range(chunks):
            tile_copy(g, k).wait_send()
    for k in range(1, layers):
        for g in range(chunks):
            sum_copy(g, k).wait_send()


def whole_rows(images, psf_taps, exposure_weights, dest_patch, dest_cell, shift_class):
    band, cols = images.shape[1:]
    bands = lax.axis_size("patch")
    layers = lax.axis_size("visit") // CORES
    owners = bands * CORES
    slots = owners * PCELLS
    image = images[0]
    above = lax.ppermute(image[band - HALO :], "patch", [(i, i + 1) for i in range(bands - 1)])
    below = lax.ppermute(image[:HALO], "patch", [(i + 1, i) for i in range(bands - 1)])
    by_cols, by_rows = lanczos_windows()
    scalars = pl.BlockSpec(memory_space=pltpu.SMEM)
    vector = pl.BlockSpec(memory_space=pltpu.VMEM)
    height = band + 2 * HALO
    anywhere = pl.BlockSpec(memory_space=pl.ANY)
    tiles, marks = pl.pallas_call(
        warp_kernel,
        out_shape=(
            jax.ShapeDtypeStruct((slots, TILE, TILE), jnp.bfloat16),
            jax.ShapeDtypeStruct((owners, PCELLS, TILE), jnp.float32),
        ),
        in_specs=[scalars] * 4 + [vector] + [anywhere] * 5,
        out_specs=(vector, vector),
        scratch_shapes=[
            pltpu.VMEM((height, cols + 3 * TILE), jnp.bfloat16),
            pltpu.VMEM((band + HALO, cols + TILE), jnp.bfloat16),
            pltpu.VMEM(by_cols.shape, jnp.bfloat16),
            pltpu.VMEM(by_rows.shape, jnp.bfloat16),
            pltpu.SMEM((2, slots), jnp.int32),
            pltpu.SemaphoreType.DMA((5,)),
        ],
        compiler_params=pltpu.CompilerParams(vmem_limit_bytes=60 * 2**20),
        cost_estimate=pl.CostEstimate(
            flops=3 * 10**9, bytes_accessed=6 * 2**20, transcendentals=0
        ),
        name="match_and_warp",
    )(
        dest_patch,
        dest_cell,
        shift_class,
        exposure_weights,
        psf_taps,
        images,
        above,
        below,
        jnp.asarray(by_cols),
        jnp.asarray(by_rows),
    )
    chunks = PCELLS // CHUNK
    dma = pltpu.SemaphoreType.DMA
    coadd, cover = pl.pallas_call(
        exchange_kernel,
        out_shape=(
            jax.ShapeDtypeStruct((PCELLS, TILE, TILE), jnp.float32),
            jax.ShapeDtypeStruct((PCELLS, TILE), jnp.float32),
        ),
        in_specs=[vector, vector],
        out_specs=(vector, vector),
        scratch_shapes=[
            pltpu.VMEM((owners, PCELLS, TILE, TILE), jnp.bfloat16),
            pltpu.VMEM((owners, PCELLS, TILE), jnp.float32),
            pltpu.VMEM((owners, PCELLS, PCELLS, TILE), jnp.float32),
            pltpu.VMEM((layers, PCELLS, TILE + PCELLS, TILE), jnp.float32),
            pltpu.VMEM((layers, PCELLS, TILE + PCELLS, TILE), jnp.float32),
            dma((chunks, owners)),
            dma((chunks, owners)),
            dma((owners,)),
            dma((owners,)),
            dma((chunks, layers)),
            dma((chunks, layers)),
            dma,
        ],
        compiler_params=pltpu.CompilerParams(
            collective_id=0, has_side_effects=True, vmem_limit_bytes=40 * 2**20
        ),
        cost_estimate=pl.CostEstimate(
            flops=10**8, bytes_accessed=6 * 2**20, transcendentals=0
        ),
        name="exchange_and_sum",
    )(tiles.reshape(owners, PCELLS, TILE, TILE), marks)
    return coadd[None], cover[:, 0][None]


def local(images, psf_taps, exposure_weights, dest_patch, dest_cell, shift_class):
    count, band, cols = images.shape
    owners = lax.axis_size("patch")
    visits = lax.axis_size("visit")
    row_of_patches = (
        count == 1
        and band == CORES * TILE
        and owners * band == PCELLS * TILE
        and cols == owners * PCELLS * TILE
        and visits == PCELLS
    )
    plan = whole_rows if row_of_patches else general
    return plan(images, psf_taps, exposure_weights, dest_patch, dest_cell, shift_class)


def solution(mesh):
    placed = (
        P("visit", "patch", None),
        P("visit", None, None),
        P("visit"),
        P("visit", "patch", None),
        P("visit", "patch", None),
        P("visit", None, "patch", None),
    )
    return jax.shard_map(
        local,
        mesh=mesh,
        in_specs=placed,
        out_specs=(P("patch", "visit", None, None), P("patch", "visit")),
        check_vma=False,
    )
```
